32 devices in a mesh: row: 8 (over y, x, core), head: 4 (over z).
Axes of the slice: x: 2, y: 2, z: 4, core: 2. Of those that a mesh axis runs over, the one named last changes fastest.
Arguments:
- features: bfloat16 [4096, 1024], P('row'), may hold values from -6 to 6
- w_qkv: bfloat16 [3, 1024, 1024], P(None, None, 'head'), may hold values from -0.1875 to 0.1875
- w_out: bfloat16 [1024, 1024], P('head'), may hold values from -0.1875 to 0.1875
- bias_gain: float32 [16], P('head'), may hold values from 0.5 to 1.5
- edge_bias: bfloat16 [64, 64, 4096], P('row'), may hold values from -6 to 250
- neighbours: int32 [64, 64], P('row'), may hold values from 0 to 63, as said below
- counts: int32 [64], P('row'), may hold values from 1 to 64, as said below
Outputs:
- mixed: bfloat16 [4096, 1024], P('row', 'head')
The draws below stay inside these ranges and needn't reach their ends.
Inputs may be any that keep to these rules, and one draw needn't show every extreme that they name: `neighbours`: key block b is owned by row device b // 8. Over all slots of the query blocks of one row device, at most 2 distinct key blocks of any one owner are named, and for every row device some owner has exactly 2. `counts`: the first query block of every row device has all 64 slots live.
All inputs are finite; a program needn't handle non-finite values.
Results may differ from the reference program's by a relative error of at most 0.011.
Values may be sent and summed in bfloat16 or wider, within the bound.
A program may use at most 256 MiB of HBM per device.

```python
import math
import jax
import jax.numpy as jnp
from jax import lax

D = 1024
HEADS = 16
HD = 64
BLK = 64
NB = 64
QB_DEV = 8
CAP = 2
NODES = 4096
QBLOCKS = 64


def plan_lists(key):
    owners = QBLOCKS // QB_DEV
    base = jax.random.fold_in(key, 7001)
    perm_keys = jax.random.split(jax.random.fold_in(base, 1), owners * owners)
    perms = jax.vmap(lambda subkey: jax.random.permutation(subkey, QB_DEV))(perm_keys)
    perms = perms.reshape(owners, owners, QB_DEV)[:, :, :CAP]
    candidate = perms + (jnp.arange(owners, dtype=jnp.int32) * QB_DEV)[None, :, None]
    candidate = candidate.reshape(owners, owners * CAP)
    picks = jax.random.randint(jax.random.fold_in(base, 2), (owners, QB_DEV, NB), 0, owners * CAP)
    forced_owner = jax.random.randint(jax.random.fold_in(base, 3), (owners,), 0, owners)
    forced = forced_owner[:, None] * CAP + jnp.arange(CAP, dtype=jnp.int32)[None, :]
    picks = picks.at[:, 0, :CAP].set(forced)
    block_ids = jnp.take_along_axis(candidate, picks.reshape(owners, QB_DEV * NB), axis=1)
    block_ids = block_ids.reshape(QBLOCKS, NB)
    levels = jax.random.randint(jax.random.fold_in(base, 4), (owners, 1), 1, NB + 1)
    raw_counts = jax.random.randint(jax.random.fold_in(base, 5), (owners, QB_DEV), 0, NB + 1)
    live_counts = jnp.maximum(levels, raw_counts)
    live_counts = live_counts.at[:, 0].set(NB)
    return (block_ids.astype(jnp.int32), live_counts.reshape(QBLOCKS).astype(jnp.int32))


def draw_neighbours(key, part):
    return plan_lists(key)[0]


def draw_counts(key, part):
    return plan_lists(key)[1]


def draw_edge_bias(key, part):
    shape = (QBLOCKS, BLK, NB * BLK)
    return jnp.clip(jax.random.normal(key, shape, jnp.float32), -6.0, 6.0).astype(jnp.bfloat16)


def block_scale(own_key, extent, shards, least, top_value):
    loudness, own = 1.0, jax.random.fold_in(own_key, 6)
    for axis_at, parts in shards:
        draws = jnp.exp(jax.random.uniform(jax.random.fold_in(own, axis_at), (parts,), jnp.float32, least / len(shards), top_value / len(shards)))
        loudness = loudness * jnp.repeat(draws, extent[axis_at] // parts).reshape([-1 if axis == axis_at else 1 for axis in range(len(extent))])
    return loudness


def scatter_about(own_key, dims, scale, bound, shards=(), kind=jnp.bfloat16):
    drawn = jax.random.normal(own_key, dims, jnp.float32) * scale
    if len(shards) > 0:
        drawn = block_scale(own_key, dims, shards, -0.22, 0.18) * drawn
    return jnp.clip(drawn, min=-bound, max=bound).astype(kind)


def setup_inputs(seed: int = 0) -> dict:
    key_list = jax.random.split(jax.random.key(seed), 8)
    features = scatter_about(key_list[0], (NODES, D), 1.0, 6.0, ((0, 8),))
    w_qkv = scatter_about(key_list[1], (3, D, HEADS * HD), D ** -0.5, 0.1875, ((2, 4),))
    w_out = scatter_about(key_list[2], (HEADS * HD, D), (HEADS * HD) ** -0.5, 0.1875, ((0, 4),))
    bias_gain = jnp.clip(jnp.exp(math.log(1.5) - 1.0986123 * jax.random.uniform(key_list[3], (HEADS,), jnp.float32) ** block_scale(key_list[3], (HEADS,), ((0, 4),), -0.2, 0.2)), 0.5, 1.5)
    edge_bias = draw_edge_bias(jax.random.fold_in(key_list[7], 71), 0)
    neighbours = draw_neighbours(jax.random.fold_in(key_list[7], 71), 0)
    counts = draw_counts(jax.random.fold_in(key_list[7], 71), 0)
    return {"features": features, "w_qkv": w_qkv, "w_out": w_out, "bias_gain": bias_gain, "edge_bias": edge_bias, "neighbours": neighbours, "counts": counts}


def reference(features, w_qkv, w_out, bias_gain, edge_bias, neighbours, counts):
    queries = jnp.dot(features, w_qkv[0], preferred_element_type=jnp.float32).astype(jnp.bfloat16)
    keys = jnp.dot(features, w_qkv[1], preferred_element_type=jnp.float32).astype(jnp.bfloat16)
    values = jnp.dot(features, w_qkv[2], preferred_element_type=jnp.float32).astype(jnp.bfloat16)
    query_blocks = queries.reshape(QBLOCKS, BLK, HEADS, HD)
    key_blocks = keys.reshape(QBLOCKS, BLK, HEADS, HD)
    value_blocks = values.reshape(QBLOCKS, BLK, HEADS, HD)
    scale = HD ** -0.5

    def one_block(inputs):
        query_tile, slot_ids, live_count, bias_tile = inputs
        near_keys = key_blocks[slot_ids].astype(jnp.float32)
        near_values = value_blocks[slot_ids].astype(jnp.float32)
        score = jnp.einsum("qhd,nkhd->hqnk", query_tile.astype(jnp.float32), near_keys) * scale
        bias_terms = bias_tile.astype(jnp.float32).reshape(BLK, NB, BLK)
        score = score + bias_gain[:, None, None, None] * bias_terms[None]
        live = jnp.arange(NB, dtype=jnp.int32) < live_count
        score = jnp.where(live[None, None, :, None], score, jnp.float32(-1e30))
        top = jnp.max(score, axis=(2, 3), keepdims=True)
        expo = jnp.exp(score - top)
        total = jnp.sum(expo, axis=(2, 3), keepdims=True)
        weights = (expo / total).astype(jnp.bfloat16)
        result = jnp.einsum("hqnk,nkhd->qhd", weights.astype(jnp.float32), near_values)
        return result.astype(jnp.bfloat16).reshape(BLK, HEADS * HD)

    attended = lax.map(one_block, (query_blocks, neighbours, counts, edge_bias))
    attended = attended.reshape(NODES, HEADS * HD)
    return jnp.dot(attended, w_out, preferred_element_type=jnp.float32).astype(jnp.bfloat16)
```

```python
import functools

import jax
import jax.numpy as jnp
from jax import lax
from jax.experimental import pallas as pl
from jax.experimental.pallas import tpu as pltpu
from jax.sharding import PartitionSpec as P

HD = 64
BLK = 64
NB = 64
HALF = BLK // 2
CAP = 2
NEG = -1e30
LOG2E = 1.4426950408889634


def swap_halves(x):
    return pltpu.roll(x, HD, 1)


def project_kernel(row_devs, req_ref, x_ref, w_ref, q_ref, *rest):
    sends, kv = rest[:row_devs], rest[row_devs]
    rows, width = kv.shape[0], w_ref.shape[2]
    x = x_ref[...]
    q = jnp.dot(x, w_ref[0], preferred_element_type=jnp.float32)
    for t in range(2):
        kv[:, t * width : (t + 1) * width] = jnp.dot(
            x, w_ref[1 + t], preferred_element_type=jnp.float32
        ).astype(jnp.bfloat16)
    q = q.reshape(rows // BLK, 2, HALF, width)
    top = q[:, 0].reshape(rows // 2, width)
    bottom = q[:, 1].reshape(rows // 2, width)
    first = lax.broadcasted_iota(jnp.int32, (rows // 2, 2 * HD), 1) < HD
    for pair in range(width // (2 * HD)):
        a = top[:, pair * 2 * HD : (pair + 1) * 2 * HD]
        b = bottom[:, pair * 2 * HD : (pair + 1) * 2 * HD]
        q_ref[2 * pair] = jnp.where(first, a, swap_halves(b)).astype(jnp.bfloat16)
        q_ref[2 * pair + 1] = jnp.where(first, swap_halves(a), b).astype(jnp.bfloat16)
    for s in range(row_devs):
        for c in range(CAP):
            at = pl.multiple_of(req_ref[s, c] * BLK, BLK)
            sends[s][c * BLK : (c + 1) * BLK, :] = kv[pl.ds(at, BLK), :]


def project(features, w_qkv, requests, row_devs):
    rows = features.shape[0]
    width = w_qkv.shape[2]
    out = [jax.ShapeDtypeStruct((width // HD, rows // 2, 2 * HD), jnp.bfloat16)]
    out += [jax.ShapeDtypeStruct((CAP * BLK, 2 * width), jnp.bfloat16)] * row_devs
    vmem = pl.BlockSpec(memory_space=pltpu.VMEM)
    return pl.pallas_call(
        functools.partial(project_kernel, row_devs),
        out_shape=out,
        in_specs=[pl.BlockSpec(memory_space=pltpu.SMEM), vmem, vmem],
        out_specs=[vmem] * len(out),
        scratch_shapes=[pltpu.VMEM((rows, 2 * width), jnp.bfloat16)],
        compiler_params=pltpu.CompilerParams(vmem_limit_bytes=40 * 2**20),
        name="project",
    )(requests, features, w_qkv)


def sums_kernel(heads, units, umap_ref, count_ref, gain_ref, bias_ref, t_ref, m_ref, tiles, best, acc):
    g = pl.program_id(0)
    count = count_ref[g]
    best[...] = jnp.full(best.shape, NEG, jnp.float32)
    acc[...] = jnp.zeros(acc.shape, jnp.float32)
    first = lax.broadcasted_iota(jnp.int32, (HALF, 2 * BLK), 1) < BLK

    def arrange(i, carry):
        for step in range(2):
            pair = i * 2 + step
            at = pl.multiple_of(pair * 2 * BLK, 2 * BLK)
            a = bias_ref[0, 0:HALF, pl.ds(at, 2 * BLK)].astype(jnp.float32)
            b = bias_ref[0, HALF:BLK, pl.ds(at, 2 * BLK)].astype(jnp.float32)
            for odd in range(2):
                j = 2 * pair + odd
                tile = jnp.where(first, swap_halves(a), b) if odd else jnp.where(first, a, swap_halves(b))
                tile = jnp.where(j < count, tile, NEG)
                tiles[j] = tile
                u = umap_ref[g, j]
                best[u] = jnp.maximum(best[u], tile)
        return carry

    lax.fori_loop(0, NB // 4, arrange, 0)
    gains = [gain_ref[h] * LOG2E for h in range(heads)]

    def add(i, carry):
        for step in range(4):
            j = i * 4 + step
            u = umap_ref[g, j]
            d = tiles[j] - best[u]
            e = [jnp.exp2(d * gains[h]) for h in range(heads)]
            for h in range(heads):
                acc[u, h] += e[h]
        return carry

    lax.fori_loop(0, (count + 3) // 4, add, 0)
    for u in range(units):
        m_ref[:, u * 2 * BLK : (u + 1) * 2 * BLK] = best[u].astype(jnp.bfloat16)
        for h in range(heads):
            t_ref[h, :, u * 2 * BLK : (u + 1) * 2 * BLK] = acc[u, h].astype(jnp.bfloat16)


def sums(umap, counts, bias_gain, edge_bias, units):
    blocks = umap.shape[0]
    heads = bias_gain.shape[0]
    wide = units * 2 * BLK
    rows2 = blocks * HALF
    grid_spec = pltpu.PrefetchScalarGridSpec(
        num_scalar_prefetch=3,
        grid=(blocks,),
        in_specs=[pl.BlockSpec((1, BLK, NB * BLK), lambda g, *_: (g, 0, 0))],
        out_specs=[
            pl.BlockSpec((heads, HALF, wide), lambda g, *_: (0, g, 0)),
            pl.BlockSpec((HALF, wide), lambda g, *_: (g, 0)),
        ],
        scratch_shapes=[
            pltpu.VMEM((NB, HALF, 2 * BLK), jnp.float32),
            pltpu.VMEM((units, HALF, 2 * BLK), jnp.float32),
            pltpu.VMEM((units, heads, HALF, 2 * BLK), jnp.float32),
        ],
    )
    return pl.pallas_call(
        functools.partial(sums_kernel, heads, units),
        out_shape=[
            jax.ShapeDtypeStruct((heads, rows2, wide), jnp.bfloat16),
            jax.ShapeDtypeStruct((rows2, wide), jnp.bfloat16),
        ],
        grid_spec=grid_spec,
        compiler_params=pltpu.CompilerParams(vmem_limit_bytes=40 * 2**20),
        cost_estimate=pl.CostEstimate(
            flops=10 * blocks * heads * BLK * NB * BLK * 100,
            bytes_accessed=12 * 2**20,
            transcendentals=blocks * heads * BLK * NB * BLK,
        ),
        name="sums",
    )(umap, counts, bias_gain, edge_bias)


def attend_kernel(row_devs, gain_ref, q_ref, t_ref, m_ref, *rest):
    got, out_ref = rest[:row_devs], rest[row_devs]
    pair = pl.program_id(0)
    units = CAP * row_devs
    rows2 = q_ref.shape[1]
    first_k = lax.broadcasted_iota(jnp.int32, (CAP * BLK, 2 * HD), 1) < HD
    first = lax.broadcasted_iota(jnp.int32, (rows2, 2 * HD), 1) < HD

    def doubled(part, odd):
        rows = []
        for s in range(row_devs):
            x = got[s][part].astype(jnp.float32)
            y = swap_halves(x)
            low = jnp.where(first_k, y if odd else x, 0.0).astype(jnp.bfloat16)
            high = jnp.where(first_k, 0.0, x if odd else y).astype(jnp.bfloat16)
            for c in range(CAP):
                rows += [low[c * BLK : (c + 1) * BLK], high[c * BLK : (c + 1) * BLK]]
        return jnp.concatenate(rows, axis=0)

    def halves(x, op, fill):
        parts = [x[:, u * 2 * BLK : (u + 1) * 2 * BLK] for u in range(units)]
        while len(parts) > 1:
            parts = [op(parts[i], parts[i + 1]) for i in range(0, len(parts) - 1, 2)] + parts[len(parts) // 2 * 2 :]
        y = parts[0]
        reduce = jnp.max if op is jnp.maximum else jnp.sum
        low = reduce(jnp.where(first, y, fill), axis=1, keepdims=True)
        high = reduce(jnp.where(first, fill, y), axis=1, keepdims=True)
        return jnp.where(first, low, high)

    outs = []
    for odd in range(2):
        gain = gain_ref[2 * pair + odd] * LOG2E
        score = lax.dot_general(
            q_ref[odd], doubled(0, odd), (((1,), (1,)), ((), ())), preferred_element_type=jnp.float32
        )
        score = score * (HD**-0.5 * LOG2E) + m_ref[...].astype(jnp.float32) * gain
        top = halves(score, jnp.maximum, -jnp.inf)
        expo = jnp.exp2(score - jnp.concatenate([top] * units, axis=1)) * t_ref[odd].astype(jnp.float32)
        total = halves(expo, jnp.add, 0.0)
        mixed = jnp.dot(expo.astype(jnp.bfloat16), doubled(1, odd), preferred_element_type=jnp.float32)
        outs.append(mixed / total)
    a, b = outs
    out_ref[0] = jnp.where(first, a, swap_halves(b)).astype(jnp.bfloat16)
    out_ref[1] = jnp.where(first, swap_halves(a), b).astype(jnp.bfloat16)


def attend(bias_gain, q, t, m, got):
    heads, rows2, _ = q.shape
    wide = m.shape[1]
    row_devs = len(got)
    grid_spec = pltpu.PrefetchScalarGridSpec(
        num_scalar_prefetch=1,
        grid=(heads // 2,),
        in_specs=[
            pl.BlockSpec((2, rows2, 2 * HD), lambda p, *_: (p, 0, 0)),
            pl.BlockSpec((2, rows2, wide), lambda p, *_: (p, 0, 0)),
            pl.BlockSpec((rows2, wide), lambda p, *_: (0, 0)),
        ]
        + [pl.BlockSpec((2, CAP * BLK, 2 * HD), lambda p, *_: (0, 0, p))] * row_devs,
        out_specs=pl.BlockSpec((2, rows2, 2 * HD), lambda p, *_: (0, 0, p)),
    )
    return pl.pallas_call(
        functools.partial(attend_kernel, row_devs),
        out_shape=jax.ShapeDtypeStruct((2, rows2, heads * HD), jnp.bfloat16),
        grid_spec=grid_spec,
        compiler_params=pltpu.CompilerParams(vmem_limit_bytes=56 * 2**20),
        name="attend",
    )(bias_gain, q, t, m, *got)


def body(features, w_qkv, w_out, bias_gain, edge_bias, neighbours, counts):
    rows = features.shape[0]
    width = w_qkv.shape[2]
    blocks = rows // BLK
    row_devs = lax.axis_size("row")
    head_devs = lax.axis_size("head")
    me = lax.axis_index("row")
    z = lax.axis_index("head")
    units = CAP * row_devs

    owner, local = neighbours // blocks, neighbours % blocks
    hit = owner[None] == jnp.arange(row_devs, dtype=jnp.int32)[:, None, None]
    low = jnp.min(jnp.where(hit, local[None], blocks - 1), axis=(1, 2))
    high = jnp.max(jnp.where(hit, local[None], 0), axis=(1, 2))
    low_here = jnp.sum(jnp.where(hit, low[:, None, None], 0), axis=0)
    hop = lax.rem(owner - me + row_devs, row_devs)
    umap = CAP * hop + (local != low_here).astype(jnp.int32)
    wanted = jnp.stack([low, high], axis=1)
    requests = lax.all_to_all(wanted, "row", 0, 0, tiled=True)
    serve = lax.rem(me - jnp.arange(row_devs, dtype=jnp.int32) + row_devs, row_devs)
    requests = jnp.sum(
        jnp.where((serve[:, None] == jnp.arange(row_devs)[None])[:, :, None], requests[None], 0), axis=1
    ).astype(jnp.int32)

    columns = w_out.shape[1] // head_devs
    w_cols = []
    for s in range(head_devs):
        piece = lax.dynamic_slice_in_dim(w_out, lax.rem(z - s + head_devs, head_devs) * columns, columns, 1)
        if s:
            piece = lax.ppermute(piece, "head", [((d + s) % head_devs, d) for d in range(head_devs)])
        w_cols.append(piece)

    q, *sends = project(features, w_qkv, requests, row_devs)
    got = [
        lax.ppermute(x, "row", [((d + s) % row_devs, d) for d in range(row_devs)]) if s else x
        for s, x in enumerate(sends)
    ]
    got = [x.reshape(CAP * BLK, 2, width).transpose(1, 0, 2) for x in got]
    t, m = sums(umap, counts, bias_gain, edge_bias, units)
    mine = attend(bias_gain, q, t, m, got)
    total = None
    for s in range(head_devs):
        x = mine
        if s:
            x = lax.ppermute(x, "head", [((d + s) % head_devs, d) for d in range(head_devs)])
        part = jnp.einsum("arc,co->aro", x, w_cols[s], preferred_element_type=jnp.float32)
        total = part if total is None else total + part
    total = total.reshape(2, blocks, HALF, columns).transpose(1, 0, 2, 3)
    return total.reshape(rows, columns).astype(jnp.bfloat16)


def solution(mesh):
    in_specs = (
        P("row", None),
        P(None, None, "head"),
        P("head", None),
        P("head"),
        P("row", None, None),
        P("row", None),
        P("row"),
    )
    return jax.shard_map(body, mesh=mesh, in_specs=in_specs, out_specs=P("row", "head"), check_vma=False)
```

```python
import functools

import jax
import jax.numpy as jnp
from jax import lax
from jax.experimental import pallas as pl
from jax.experimental.pallas import tpu as pltpu
from jax.sharding import PartitionSpec as P

HD = 64
BLK = 64
NB = 64
HALF = BLK // 2
CAP = 2
NEG = -1e30
LOG2E = 1.4426950408889634


def swap_halves(x):
    return pltpu.roll(x, HD, 1)


MESH = pl.DeviceIdType.MESH


def greet(peers):
    barrier = pltpu.get_barrier_semaphore()
    for peer in peers:
        pl.semaphore_signal(barrier, inc=1, device_id=peer, device_id_type=MESH)
    pl.semaphore_wait(barrier, len(peers))


def exchange_kernel(
    row_devs, head_devs, want_ref, x_hbm, w_hbm, wout_ref, q_ref, got_ref, wcol_ref,
    x_ref, w_ref, kv, reqs, sends, load_sem, req_send, req_recv, kv_send, kv_recv, w_send, w_recv,
):
    loads = [
        pltpu.make_async_copy(x_hbm, x_ref, load_sem.at[0]),
        pltpu.make_async_copy(w_hbm, w_ref, load_sem.at[1]),
    ]
    for load in loads:
        load.start()
    me, z = lax.axis_index("row"), lax.axis_index("head")
    rows, width = x_ref.shape[0], w_ref.shape[2]
    columns = wcol_ref.shape[2]

    def row_peer(s):
        return {"row": lax.rem(me + s + row_devs, row_devs)}

    def head_peer(s):
        return {"head": lax.rem(z + s + head_devs, head_devs)}

    greet([row_peer(s) for s in range(1, row_devs)] + [head_peer(s) for s in range(1, head_devs)])
    asks, moves = [None], [None]
    for s in range(1, row_devs):
        asks.append(
            pltpu.make_async_remote_copy(
                want_ref.at[s], reqs.at[s], req_send.at[s], req_recv.at[s], device_id=row_peer(s), device_id_type=MESH
            )
        )
        asks[s].start()
    for s in range(1, head_devs):
        at = pl.multiple_of(lax.rem(z - s + head_devs, head_devs) * columns, columns)
        moves.append(
            pltpu.make_async_remote_copy(
                wout_ref.at[:, pl.ds(at, columns)], wcol_ref.at[s], w_send.at[s], w_recv.at[s],
                device_id=head_peer(-s), device_id_type=MESH,
            )
        )
        moves[s].start()
    wcol_ref[0] = wout_ref[:, pl.ds(pl.multiple_of(z * columns, columns), columns)]

    for load in loads:
        load.wait()
    x = x_ref[...]
    for t in range(2):
        kv[t] = jnp.dot(x, w_ref[1 + t], preferred_element_type=jnp.float32).astype(jnp.bfloat16)

    column = lax.broadcasted_iota(jnp.int32, (BLK, rows), 1)
    row = lax.broadcasted_iota(jnp.int32, (BLK, rows), 0)

    def pick(ref, s, dst):
        for c in range(CAP):
            start = jnp.concatenate([ref[s, c : c + 1, :]] * (rows // 128), axis=1)
            hot = (column == start * BLK + row).astype(jnp.float32).astype(jnp.bfloat16)
            for t in range(2):
                dst[s, t, c * BLK : (c + 1) * BLK, :] = jnp.dot(
                    hot, kv[t], preferred_element_type=jnp.float32
                ).astype(jnp.bfloat16)

    copies = [None]
    for s in range(1, row_devs):
        asks[s].wait_recv()
        pick(reqs, s, sends)
        copies.append(
            pltpu.make_async_remote_copy(
                sends.at[s], got_ref.at[s], kv_send.at[s], kv_recv.at[s], device_id=row_peer(-s), device_id_type=MESH
            )
        )
        copies[s].start()
    pick(want_ref, 0, got_ref)

    q = jnp.dot(x, w_ref[0], preferred_element_type=jnp.float32).reshape(rows // BLK, 2, HALF, width)
    top = q[:, 0].reshape(rows // 2, width)
    bottom = q[:, 1].reshape(rows // 2, width)
    first = lax.broadcasted_iota(jnp.int32, (rows // 2, 2 * HD), 1) < HD
    for pair in range(width // (2 * HD)):
        a = top[:, pair * 2 * HD : (pair + 1) * 2 * HD]
        b = bottom[:, pair * 2 * HD : (pair + 1) * 2 * HD]
        q_ref[2 * pair] = jnp.where(first, a, swap_halves(b)).astype(jnp.bfloat16)
        q_ref[2 * pair + 1] = jnp.where(first, swap_halves(a), b).astype(jnp.bfloat16)

    for s in range(1, row_devs):
        asks[s].wait_send()
        copies[s].wait()
    for s in range(1, head_devs):
        moves[s].wait()


def exchange(want, features, w_qkv, w_out, row_devs, head_devs):
    rows, depth = features.shape
    width = w_qkv.shape[2]
    vmem = pl.BlockSpec(memory_space=pltpu.VMEM)
    anywhere = pl.BlockSpec(memory_space=pl.ANY)
    dma = pltpu.SemaphoreType.DMA
    return pl.pallas_call(
        functools.partial(exchange_kernel, row_devs, head_devs),
        out_shape=[
            jax.ShapeDtypeStruct((width // HD, rows // 2, 2 * HD), jnp.bfloat16),
            jax.ShapeDtypeStruct((row_devs, 2, CAP * BLK, width), jnp.bfloat16),
            jax.ShapeDtypeStruct((head_devs, w_out.shape[0], w_out.shape[1] // head_devs), jnp.bfloat16),
        ],
        in_specs=[vmem, anywhere, anywhere, vmem],
        out_specs=[vmem] * 3,
        scratch_shapes=[
            pltpu.VMEM((rows, depth), jnp.bfloat16),
            pltpu.VMEM(w_qkv.shape, jnp.bfloat16),
            pltpu.VMEM((2, rows, width), jnp.bfloat16),
            pltpu.VMEM((row_devs, 8, 128), jnp.int32),
            pltpu.VMEM((row_devs, 2, CAP * BLK, width), jnp.bfloat16),
            dma((2,)),
            dma((row_devs,)),
            dma((row_devs,)),
            dma((row_devs,)),
            dma((row_devs,)),
            dma((head_devs,)),
            dma((head_devs,)),
        ],
        compiler_params=pltpu.CompilerParams(
            vmem_limit_bytes=40 * 2**20, collective_id=0, has_side_effects=True
        ),
        name="exchange",
    )(want, features, w_qkv, w_out)


def sums_kernel(heads, units, umap_ref, count_ref, gain_ref, bias_ref, t_ref, m_ref, tiles, best, acc):
    g = pl.program_id(0)
    count = count_ref[g]
    best[...] = jnp.full(best.shape, NEG, jnp.float32)
    acc[...] = jnp.zeros(acc.shape, jnp.float32)
    first = lax.broadcasted_iota(jnp.int32, (HALF, 2 * BLK), 1) < BLK

    def arrange(i, carry):
        for step in range(2):
            pair = i * 2 + step
            at = pl.multiple_of(pair * 2 * BLK, 2 * BLK)
            a = bias_ref[0, 0:HALF, pl.ds(at, 2 * BLK)].astype(jnp.float32)
            b = bias_ref[0, HALF:BLK, pl.ds(at, 2 * BLK)].astype(jnp.float32)
            for odd in range(2):
                j = 2 * pair + odd
                tile = jnp.where(first, swap_halves(a), b) if odd else jnp.where(first, a, swap_halves(b))
                tile = jnp.where(j < count, tile, NEG)
                tiles[j] = tile
                u = umap_ref[g, j]
                best[u] = jnp.maximum(best[u], tile)
        return carry

    lax.fori_loop(0, NB // 4, arrange, 0)
    gains = [gain_ref[h] * LOG2E for h in range(heads)]

    def add(i, carry):
        for step in range(4):
            j = i * 4 + step
            u = umap_ref[g, j]
            d = tiles[j] - best[u]
            e = [jnp.exp2(d * gains[h]) for h in range(heads)]
            for h in range(heads):
                acc[u, h] += e[h]
        return carry

    lax.fori_loop(0, (count + 3) // 4, add, 0)
    for u in range(units):
        m_ref[:, u * 2 * BLK : (u + 1) * 2 * BLK] = best[u].astype(jnp.bfloat16)
        for h in range(heads):
            t_ref[h, :, u * 2 * BLK : (u + 1) * 2 * BLK] = acc[u, h].astype(jnp.bfloat16)


def sums(umap, counts, bias_gain, edge_bias, units):
    blocks = umap.shape[0]
    heads = bias_gain.shape[0]
    wide = units * 2 * BLK
    rows2 = blocks * HALF
    grid_spec = pltpu.PrefetchScalarGridSpec(
        num_scalar_prefetch=3,
        grid=(blocks,),
        in_specs=[pl.BlockSpec((1, BLK, NB * BLK), lambda g, *_: (g, 0, 0))],
        out_specs=[
            pl.BlockSpec((heads, HALF, wide), lambda g, *_: (0, g, 0)),
            pl.BlockSpec((HALF, wide), lambda g, *_: (g, 0)),
        ],
        scratch_shapes=[
            pltpu.VMEM((NB, HALF, 2 * BLK), jnp.float32),
            pltpu.VMEM((units, HALF, 2 * BLK), jnp.float32),
            pltpu.VMEM((units, heads, HALF, 2 * BLK), jnp.float32),
        ],
    )
    return pl.pallas_call(
        functools.partial(sums_kernel, heads, units),
        out_shape=[
            jax.ShapeDtypeStruct((heads, rows2, wide), jnp.bfloat16),
            jax.ShapeDtypeStruct((rows2, wide), jnp.bfloat16),
        ],
        grid_spec=grid_spec,
        compiler_params=pltpu.CompilerParams(vmem_limit_bytes=40 * 2**20),
        cost_estimate=pl.CostEstimate(
            flops=10 * blocks * heads * BLK * NB * BLK * 100,
            bytes_accessed=12 * 2**20,
            transcendentals=blocks * heads * BLK * NB * BLK,
        ),
        name="sums",
    )(umap, counts, bias_gain, edge_bias)


def attend_kernel(
    row_devs, head_devs, gain_ref, q_ref, t_ref, m_ref, got_ref, wcol_ref, out_ref, att, send_sem, recv_sem
):
    z = lax.axis_index("head")
    peers = [{"head": lax.rem(z + s, head_devs)} for s in range(head_devs)]
    greet(peers[1:])
    units = CAP * row_devs
    rows2 = q_ref.shape[1]
    first_k = lax.broadcasted_iota(jnp.int32, (CAP * BLK, 2 * HD), 1) < HD
    first = lax.broadcasted_iota(jnp.int32, (rows2, 2 * HD), 1) < HD

    def doubled(part, pair, odd):
        rows = []
        for s in range(row_devs):
            x = got_ref[s, part, :, pair * 2 * HD : (pair + 1) * 2 * HD].astype(jnp.float32)
            y = swap_halves(x)
            low = jnp.where(first_k, y if odd else x, 0.0).astype(jnp.bfloat16)
            high = jnp.where(first_k, 0.0, x if odd else y).astype(jnp.bfloat16)
            for c in range(CAP):
                rows += [low[c * BLK : (c + 1) * BLK], high[c * BLK : (c + 1) * BLK]]
        return jnp.concatenate(rows, axis=0)

    def halves(x, op, fill):
        parts = [x[:, u * 2 * BLK : (u + 1) * 2 * BLK] for u in range(units)]
        while len(parts) > 1:
            parts = [op(parts[i], parts[i + 1]) for i in range(0, len(parts) - 1, 2)] + parts[len(parts) // 2 * 2 :]
        y = parts[0]
        reduce = jnp.max if op is jnp.maximum else jnp.sum
        low = reduce(jnp.where(first, y, fill), axis=1, keepdims=True)
        high = reduce(jnp.where(first, fill, y), axis=1, keepdims=True)
        return jnp.where(first, low, high)

    copies = []
    for pair in range(q_ref.shape[0] // 2):
        outs = []
        for odd in range(2):
            h = 2 * pair + odd
            gain = gain_ref[h] * LOG2E
            score = lax.dot_general(
                q_ref[h], doubled(0, pair, odd), (((1,), (1,)), ((), ())), preferred_element_type=jnp.float32
            )
            score = score * (HD**-0.5 * LOG2E) + m_ref[...].astype(jnp.float32) * gain
            top = halves(score, jnp.maximum, -jnp.inf)
            expo = jnp.exp2(score - jnp.concatenate([top] * units, axis=1)) * t_ref[h].astype(jnp.float32)
            total = halves(expo, jnp.add, 0.0)
            mixed = jnp.dot(expo.astype(jnp.bfloat16), doubled(1, pair, odd), preferred_element_type=jnp.float32)
            outs.append(mixed / total)
        a, b = outs
        lanes = slice(pair * 2 * HD, (pair + 1) * 2 * HD)
        att[0, 0, :, lanes] = jnp.where(first, a, swap_halves(b)).astype(jnp.bfloat16)
        att[0, 1, :, lanes] = jnp.where(first, swap_halves(a), b).astype(jnp.bfloat16)
        for s in range(1, head_devs):
            here = pl.ds(pair * 2 * HD, 2 * HD)
            copy = pltpu.make_async_remote_copy(
                att.at[0, :, :, here],
                att.at[s, :, :, here],
                send_sem.at[pair, s],
                recv_sem.at[pair, s],
                device_id=peers[head_devs - s],
                device_id_type=MESH,
            )
            copy.start()
            copies.append((s, copy))
    blocks, columns = out_ref.shape[0], out_ref.shape[3]
    total = [None, None]
    for s in range(head_devs):
        for shift, copy in copies:
            if shift == s:
                copy.wait_recv()
        for side in range(2):
            part = jnp.dot(att[s, side], wcol_ref[s], preferred_element_type=jnp.float32)
            total[side] = part if s == 0 else total[side] + part
    for side in range(2):
        out_ref[:, side] = total[side].reshape(blocks, HALF, columns).astype(jnp.bfloat16)
    for _, copy in copies:
        copy.wait_send()


def attend(bias_gain, q, t, m, got, wcol):
    heads, rows2, _ = q.shape
    head_devs, _, columns = wcol.shape
    vmem = pl.BlockSpec(memory_space=pltpu.VMEM)
    return pl.pallas_call(
        functools.partial(attend_kernel, got.shape[0], head_devs),
        out_shape=jax.ShapeDtypeStruct((rows2 // HALF, 2, HALF, columns), jnp.bfloat16),
        in_specs=[pl.BlockSpec(memory_space=pltpu.SMEM)] + [vmem] * 5,
        out_specs=vmem,
        scratch_shapes=[
            pltpu.VMEM((head_devs, 2, rows2, heads * HD), jnp.bfloat16),
            pltpu.SemaphoreType.DMA((heads // 2, head_devs)),
            pltpu.SemaphoreType.DMA((heads // 2, head_devs)),
        ],
        compiler_params=pltpu.CompilerParams(
            vmem_limit_bytes=56 * 2**20, collective_id=1, has_side_effects=True
        ),
        name="attend",
    )(bias_gain, q, t, m, got, wcol)


def body(features, w_qkv, w_out, bias_gain, edge_bias, neighbours, counts):
    rows = features.shape[0]
    blocks = rows // BLK
    row_devs = lax.axis_size("row")
    head_devs = lax.axis_size("head")
    me = lax.axis_index("row")
    units = CAP * row_devs

    owner, local = neighbours // blocks, neighbours % blocks
    hop = lax.rem(owner - me + row_devs, row_devs)
    hit = hop[None] == jnp.arange(row_devs, dtype=jnp.int32)[:, None, None]
    low = jnp.min(jnp.where(hit, local[None], blocks - 1), axis=(1, 2))
    high = jnp.max(jnp.where(hit, local[None], 0), axis=(1, 2))
    low_here = jnp.sum(jnp.where(hit, low[:, None, None], 0), axis=0)
    umap = CAP * hop + (local != low_here).astype(jnp.int32)
    wanted = jnp.stack([low, high], axis=1)
    want = jnp.broadcast_to(jnp.pad(wanted, ((0, 0), (0, 6)))[:, :, None], (row_devs, 8, 128))
    q, got, wcol = exchange(want, features, w_qkv, w_out, row_devs, head_devs)
    t, m = sums(umap, counts, bias_gain, edge_bias, units)
    out = attend(bias_gain, q, t, m, got, wcol)
    return out.reshape(rows, out.shape[3])


def solution(mesh):
    in_specs = (
        P("row", None),
        P(None, None, "head"),
        P("head", None),
        P("head"),
        P("row", None, None),
        P("row", None),
        P("row"),
    )
    return jax.shard_map(body, mesh=mesh, in_specs=in_specs, out_specs=P("row", "head"), check_vma=False)
```

```python
import functools

import jax
import jax.numpy as jnp
from jax import lax
from jax.experimental import pallas as pl
from jax.experimental.pallas import tpu as pltpu
from jax.sharding import PartitionSpec as P

HD = 64
BLK = 64
NB = 64
HALF = BLK // 2
CAP = 2
NEG = -1e30
LOG2E = 1.4426950408889634


def swap_halves(x):
    return pltpu.roll(x, HD, 1)


MESH = pl.DeviceIdType.MESH


def greet(peers):
    barrier = pltpu.get_barrier_semaphore()
    for peer in peers:
        pl.semaphore_signal(barrier, inc=1, device_id=peer, device_id_type=MESH)
    pl.semaphore_wait(barrier, len(peers))


def exchange_kernel(
    row_devs, head_devs, want_ref, x_hbm, w_hbm, wout_ref, q_ref, got_ref, wcol_ref,
    x_ref, w_ref, kv, reqs, sends, load_sem, req_send, req_recv, kv_send, kv_recv, w_send, w_recv,
):
    loads = [
        pltpu.make_async_copy(x_hbm, x_ref, load_sem.at[0]),
        pltpu.make_async_copy(w_hbm, w_ref, load_sem.at[1]),
    ]
    for load in loads:
        load.start()
    me, z = lax.axis_index("row"), lax.axis_index("head")
    rows, width = x_ref.shape[0], w_ref.shape[2]
    columns = wcol_ref.shape[2]

    def row_peer(s):
        return {"row": lax.rem(me + s + row_devs, row_devs)}

    def head_peer(s):
        return {"head": lax.rem(z + s + head_devs, head_devs)}

    greet([row_peer(s) for s in range(1, row_devs)] + [head_peer(s) for s in range(1, head_devs)])
    asks, moves = [None], [None]
    for s in range(1, row_devs):
        asks.append(
            pltpu.make_async_remote_copy(
                want_ref.at[s], reqs.at[s], req_send.at[s], req_recv.at[s], device_id=row_peer(s), device_id_type=MESH
            )
        )
        asks[s].start()
    for s in range(1, head_devs):
        at = pl.multiple_of(lax.rem(z - s + head_devs, head_devs) * columns, columns)
        moves.append(
            pltpu.make_async_remote_copy(
                wout_ref.at[:, pl.ds(at, columns)], wcol_ref.at[s], w_send.at[s], w_recv.at[s],
                device_id=head_peer(-s), device_id_type=MESH,
            )
        )
        moves[s].start()
    wcol_ref[0] = wout_ref[:, pl.ds(pl.multiple_of(z * columns, columns), columns)]

    for load in loads:
        load.wait()
    x = x_ref[...]
    for t in range(2):
        kv[t] = jnp.dot(x, w_ref[1 + t], preferred_element_type=jnp.float32).astype(jnp.bfloat16)

    column = lax.broadcasted_iota(jnp.int32, (BLK, rows), 1)
    row = lax.broadcasted_iota(jnp.int32, (BLK, rows), 0)

    def pick(ref, s, dst):
        for c in range(CAP):
            start = jnp.concatenate([ref[s, c : c + 1, :]] * (rows // 128), axis=1)
            hot = (column == start * BLK + row).astype(jnp.float32).astype(jnp.bfloat16)
            for t in range(2):
                dst[s, t, c * BLK : (c + 1) * BLK, :] = jnp.dot(
                    hot, kv[t], preferred_element_type=jnp.float32
                ).astype(jnp.bfloat16)

    copies = [None]
    for s in range(1, row_devs):
        asks[s].wait_recv()
        pick(reqs, s, sends)
        copies.append(
            pltpu.make_async_remote_copy(
                sends.at[s], got_ref.at[s], kv_send.at[s], kv_recv.at[s], device_id=row_peer(-s), device_id_type=MESH
            )
        )
        copies[s].start()
    pick(want_ref, 0, got_ref)

    q = jnp.dot(x, w_ref[0], preferred_element_type=jnp.float32).reshape(rows // BLK, 2, HALF, width)
    top = q[:, 0].reshape(rows // 2, width)
    bottom = q[:, 1].reshape(rows // 2, width)
    first = lax.broadcasted_iota(jnp.int32, (rows // 2, 2 * HD), 1) < HD
    for pair in range(width // (2 * HD)):
        a = top[:, pair * 2 * HD : (pair + 1) * 2 * HD]
        b = bottom[:, pair * 2 * HD : (pair + 1) * 2 * HD]
        q_ref[2 * pair] = jnp.where(first, a, swap_halves(b)).astype(jnp.bfloat16)
        q_ref[2 * pair + 1] = jnp.where(first, swap_halves(a), b).astype(jnp.bfloat16)

    for s in range(1, row_devs):
        asks[s].wait_send()
        copies[s].wait()
    for s in range(1, head_devs):
        moves[s].wait()


def exchange(want, features, w_qkv, w_out, row_devs, head_devs):
    rows, depth = features.shape
    width = w_qkv.shape[2]
    vmem = pl.BlockSpec(memory_space=pltpu.VMEM)
    anywhere = pl.BlockSpec(memory_space=pltpu.HBM)
    dma = pltpu.SemaphoreType.DMA
    return pl.pallas_call(
        functools.partial(exchange_kernel, row_devs, head_devs),
        out_shape=[
            jax.ShapeDtypeStruct((width // HD, rows // 2, 2 * HD), jnp.bfloat16),
            jax.ShapeDtypeStruct((row_devs, 2, CAP * BLK, width), jnp.bfloat16),
            jax.ShapeDtypeStruct((head_devs, w_out.shape[0], w_out.shape[1] // head_devs), jnp.bfloat16),
        ],
        in_specs=[vmem, anywhere, anywhere, vmem],
        out_specs=[vmem] * 3,
        scratch_shapes=[
            pltpu.VMEM((rows, depth), jnp.bfloat16),
            pltpu.VMEM(w_qkv.shape, jnp.bfloat16),
            pltpu.VMEM((2, rows, width), jnp.bfloat16),
            pltpu.VMEM((row_devs, 8, 128), jnp.int32),
            pltpu.VMEM((row_devs, 2, CAP * BLK, width), jnp.bfloat16),
            dma((2,)),
            dma((row_devs,)),
            dma((row_devs,)),
            dma((row_devs,)),
            dma((row_devs,)),
            dma((head_devs,)),
            dma((head_devs,)),
        ],
        compiler_params=pltpu.CompilerParams(
            vmem_limit_bytes=60 * 2**20, collective_id=0, has_side_effects=True
        ),
        name="exchange",
    )(want, features, w_qkv, w_out)


def sums_kernel(heads, units, umap_ref, count_ref, gain_ref, bias_ref, t_ref, m_ref, tiles, best, acc):
    g = pl.program_id(0)
    count = count_ref[g]
    best[...] = jnp.full(best.shape, NEG, jnp.float32)
    acc[...] = jnp.zeros(acc.shape, jnp.float32)
    first = lax.broadcasted_iota(jnp.int32, (HALF, 2 * BLK), 1) < BLK

    def arrange(i, carry):
        for step in range(2):
            pair = i * 2 + step
            at = pl.multiple_of(pair * 2 * BLK, 2 * BLK)
            a = bias_ref[0, 0:HALF, pl.ds(at, 2 * BLK)].astype(jnp.float32)
            b = bias_ref[0, HALF:BLK, pl.ds(at, 2 * BLK)].astype(jnp.float32)
            for odd in range(2):
                j = 2 * pair + odd
                tile = jnp.where(first, swap_halves(a), b) if odd else jnp.where(first, a, swap_halves(b))
                tile = jnp.where(j < count, tile, NEG)
                tiles[j] = tile
                u = umap_ref[g, j]
                best[u] = jnp.maximum(best[u], tile)
        return carry

    lax.fori_loop(0, NB // 4, arrange, 0)
    gains = [gain_ref[h] * LOG2E for h in range(heads)]

    def add(i, carry):
        for step in range(4):
            j = i * 4 + step
            u = umap_ref[g, j]
            d = tiles[j] - best[u]
            e = [jnp.exp2(d * gains[h]) for h in range(heads)]
            for h in range(heads):
                acc[u, h] += e[h]
        return carry

    lax.fori_loop(0, (count + 3) // 4, add, 0)
    for u in range(units):
        m_ref[:, u * 2 * BLK : (u + 1) * 2 * BLK] = best[u].astype(jnp.bfloat16)
        for h in range(heads):
            t_ref[h, :, u * 2 * BLK : (u + 1) * 2 * BLK] = acc[u, h].astype(jnp.bfloat16)


def sums(umap, counts, bias_gain, edge_bias, units):
    blocks = umap.shape[0]
    heads = bias_gain.shape[0]
    wide = units * 2 * BLK
    rows2 = blocks * HALF
    grid_spec = pltpu.PrefetchScalarGridSpec(
        num_scalar_prefetch=3,
        grid=(blocks,),
        in_specs=[pl.BlockSpec((1, BLK, NB * BLK), lambda g, *_: (g, 0, 0))],
        out_specs=[
            pl.BlockSpec((heads, HALF, wide), lambda g, *_: (0, g, 0)),
            pl.BlockSpec((HALF, wide), lambda g, *_: (g, 0)),
        ],
        scratch_shapes=[
            pltpu.VMEM((NB, HALF, 2 * BLK), jnp.float32),
            pltpu.VMEM((units, HALF, 2 * BLK), jnp.float32),
            pltpu.VMEM((units, heads, HALF, 2 * BLK), jnp.float32),
        ],
    )
    return pl.pallas_call(
        functools.partial(sums_kernel, heads, units),
        out_shape=[
            jax.ShapeDtypeStruct((heads, rows2, wide), jnp.bfloat16),
            jax.ShapeDtypeStruct((rows2, wide), jnp.bfloat16),
        ],
        grid_spec=grid_spec,
        compiler_params=pltpu.CompilerParams(vmem_limit_bytes=60 * 2**20),
        cost_estimate=pl.CostEstimate(
            flops=10 * blocks * heads * BLK * NB * BLK * 100,
            bytes_accessed=12 * 2**20,
            transcendentals=blocks * heads * BLK * NB * BLK,
        ),
        name="sums",
    )(umap, counts, bias_gain, edge_bias)


def attend_kernel(
    row_devs, head_devs, gain_ref, q_ref, t_ref, m_ref, got_ref, wcol_ref, out_ref, att, send_sem, recv_sem
):
    z = lax.axis_index("head")
    peers = [{"head": lax.rem(z + s, head_devs)} for s in range(head_devs)]
    greet(peers[1:])
    units = CAP * row_devs
    rows2 = q_ref.shape[1]
    first_k = lax.broadcasted_iota(jnp.int32, (CAP * BLK, 2 * HD), 1) < HD
    first = lax.broadcasted_iota(jnp.int32, (rows2, 2 * HD), 1) < HD

    def doubled(part, pair, odd):
        rows = []
        for s in range(row_devs):
            x = got_ref[s, part, :, pair * 2 * HD : (pair + 1) * 2 * HD].astype(jnp.float32)
            y = swap_halves(x)
            low = jnp.where(first_k, y if odd else x, 0.0).astype(jnp.bfloat16)
            high = jnp.where(first_k, 0.0, x if odd else y).astype(jnp.bfloat16)
            for c in range(CAP):
                rows += [low[c * BLK : (c + 1) * BLK], high[c * BLK : (c + 1) * BLK]]
        return jnp.concatenate(rows, axis=0)

    def halves(x, op, fill):
        parts = [x[:, u * 2 * BLK : (u + 1) * 2 * BLK] for u in range(units)]
        while len(parts) > 1:
            parts = [op(parts[i], parts[i + 1]) for i in range(0, len(parts) - 1, 2)] + parts[len(parts) // 2 * 2 :]
        y = parts[0]
        reduce = jnp.max if op is jnp.maximum else jnp.sum
        low = reduce(jnp.where(first, y, fill), axis=1, keepdims=True)
        high = reduce(jnp.where(first, fill, y), axis=1, keepdims=True)
        return jnp.where(first, low, high)

    copies = []
    for pair in range(q_ref.shape[0] // 2):
        outs = []
        for odd in range(2):
            h = 2 * pair + odd
            gain = gain_ref[h] * LOG2E
            score = lax.dot_general(
                q_ref[h], doubled(0, pair, odd), (((1,), (1,)), ((), ())), preferred_element_type=jnp.float32
            )
            score = score * (HD**-0.5 * LOG2E) + m_ref[...].astype(jnp.float32) * gain
            top = halves(score, jnp.maximum, -jnp.inf)
            expo = jnp.exp2(score - jnp.concatenate([top] * units, axis=1)) * t_ref[h].astype(jnp.float32)
            total = halves(expo, jnp.add, 0.0)
            mixed = jnp.dot(expo.astype(jnp.bfloat16), doubled(1, pair, odd), preferred_element_type=jnp.float32)
            outs.append(mixed / total)
        a, b = outs
        lanes = slice(pair * 2 * HD, (pair + 1) * 2 * HD)
        att[0, 0, :, lanes] = jnp.where(first, a, swap_halves(b)).astype(jnp.bfloat16)
        att[0, 1, :, lanes] = jnp.where(first, swap_halves(a), b).astype(jnp.bfloat16)
        for s in range(1, head_devs):
            here = pl.ds(pair * 2 * HD, 2 * HD)
            copy = pltpu.make_async_remote_copy(
                att.at[0, :, :, here],
                att.at[s, :, :, here],
                send_sem.at[pair, s],
                recv_sem.at[pair, s],
                device_id=peers[head_devs - s],
                device_id_type=MESH,
            )
            copy.start()
            copies.append((s, copy))
    blocks, columns = out_ref.shape[0], out_ref.shape[3]
    total = [None, None]
    for s in range(head_devs):
        for shift, copy in copies:
            if shift == s:
                copy.wait_recv()
        for side in range(2):
            part = jnp.dot(att[s, side], wcol_ref[s], preferred_element_type=jnp.float32)
            total[side] = part if s == 0 else total[side] + part
    for side in range(2):
        out_ref[:, side] = total[side].reshape(blocks, HALF, columns).astype(jnp.bfloat16)
    for _, copy in copies:
        copy.wait_send()


def attend(bias_gain, q, t, m, got, wcol):
    heads, rows2, _ = q.shape
    head_devs, _, columns = wcol.shape
    vmem = pl.BlockSpec(memory_space=pltpu.VMEM)
    return pl.pallas_call(
        functools.partial(attend_kernel, got.shape[0], head_devs),
        out_shape=jax.ShapeDtypeStruct((rows2 // HALF, 2, HALF, columns), jnp.bfloat16),
        in_specs=[pl.BlockSpec(memory_space=pltpu.SMEM)] + [vmem] * 5,
        out_specs=vmem,
        scratch_shapes=[
            pltpu.VMEM((head_devs, 2, rows2, heads * HD), jnp.bfloat16),
            pltpu.SemaphoreType.DMA((heads // 2, head_devs)),
            pltpu.SemaphoreType.DMA((heads // 2, head_devs)),
        ],
        compiler_params=pltpu.CompilerParams(
            vmem_limit_bytes=60 * 2**20, collective_id=1, has_side_effects=True
        ),
        name="attend",
    )(bias_gain, q, t, m, got, wcol)


def body(features, w_qkv, w_out, bias_gain, edge_bias, neighbours, counts):
    rows = features.shape[0]
    blocks = rows // BLK
    row_devs = lax.axis_size("row")
    head_devs = lax.axis_size("head")
    me = lax.axis_index("row")
    units = CAP * row_devs

    owner, local = neighbours // blocks, neighbours % blocks
    hop = lax.rem(owner - me + row_devs, row_devs)
    hit = hop[None] == jnp.arange(row_devs, dtype=jnp.int32)[:, None, None]
    low = jnp.min(jnp.where(hit, local[None], blocks - 1), axis=(1, 2))
    high = jnp.max(jnp.where(hit, local[None], 0), axis=(1, 2))
    low_here = jnp.sum(jnp.where(hit, low[:, None, None], 0), axis=0)
    umap = CAP * hop + (local != low_here).astype(jnp.int32)
    wanted = jnp.stack([low, high], axis=1)
    want = jnp.broadcast_to(jnp.pad(wanted, ((0, 0), (0, 6)))[:, :, None], (row_devs, 8, 128))
    q, got, wcol = exchange(want, features, w_qkv, w_out, row_devs, head_devs)
    t, m = sums(umap, counts, bias_gain, edge_bias, units)
    out = attend(bias_gain, q, t, m, got, wcol)
    return out.reshape(rows, out.shape[3])


def solution(mesh):
    in_specs = (
        P("row", None),
        P(None, None, "head"),
        P("head", None),
        P("head"),
        P("row", None, None),
        P("row", None),
        P("row"),
    )
    return jax.shard_map(body, mesh=mesh, in_specs=in_specs, out_specs=P("row", "head"), check_vma=False)
```

```python
import functools

import jax
import jax.numpy as jnp
from jax import lax
from jax.experimental import pallas as pl
from jax.experimental.pallas import tpu as pltpu
from jax.sharding import PartitionSpec as P

HD = 64
BLK = 64
NB = 64
HALF = BLK // 2
CAP = 2
NEG = -1e30
LOG2E = 1.4426950408889634


def swap_halves(x):
    return pltpu.roll(x, HD, 1)


MESH = pl.DeviceIdType.MESH


def greet(peers):
    barrier = pltpu.get_barrier_semaphore()
    for peer in peers:
        pl.semaphore_signal(barrier, inc=1, device_id=peer, device_id_type=MESH)
    pl.semaphore_wait(barrier, len(peers))


def exchange_kernel(
    row_devs, head_devs, want_ref, x_hbm, w_hbm, wout_ref, q_ref, got_ref, wcol_ref,
    x_ref, w_ref, kv, reqs, sends, load_sem, req_send, req_recv, kv_send, kv_recv, w_send, w_recv,
):
    loads = [
        pltpu.make_async_copy(x_hbm, x_ref, load_sem.at[0]),
        pltpu.make_async_copy(w_hbm, w_ref, load_sem.at[1]),
    ]
    for load in loads:
        load.start()
    me, z = lax.axis_index("row"), lax.axis_index("head")
    rows, width = x_ref.shape[0], w_ref.shape[2]
    columns = wcol_ref.shape[2]

    def row_peer(s):
        return {"row": lax.rem(me + s + row_devs, row_devs)}

    def head_peer(s):
        return {"head": lax.rem(z + s + head_devs, head_devs)}

    greet([row_peer(s) for s in range(1, row_devs)] + [head_peer(s) for s in range(1, head_devs)])
    asks, moves = [None], [None]
    for s in range(1, row_devs):
        asks.append(
            pltpu.make_async_remote_copy(
                want_ref.at[s], reqs.at[s], req_send.at[s], req_recv.at[s], device_id=row_peer(s), device_id_type=MESH
            )
        )
        asks[s].start()
    for s in range(1, head_devs):
        at = pl.multiple_of(lax.rem(z - s + head_devs, head_devs) * columns, columns)
        moves.append(
            pltpu.make_async_remote_copy(
                wout_ref.at[:, pl.ds(at, columns)], wcol_ref.at[s], w_send.at[s], w_recv.at[s],
                device_id=head_peer(-s), device_id_type=MESH,
            )
        )
        moves[s].start()
    wcol_ref[0] = wout_ref[:, pl.ds(pl.multiple_of(z * columns, columns), columns)]

    for load in loads:
        load.wait()
    x = x_ref[...]
    for t in range(2):
        kv[t] = jnp.dot(x, w_ref[1 + t], preferred_element_type=jnp.float32).astype(jnp.bfloat16)

    column = lax.broadcasted_iota(jnp.int32, (BLK, rows), 1)
    row = lax.broadcasted_iota(jnp.int32, (BLK, rows), 0)

    def pick(ref, s, dst):
        for c in range(CAP):
            start = jnp.concatenate([ref[s, c : c + 1, :]] * (rows // 128), axis=1)
            hot = (column == start * BLK + row).astype(jnp.float32).astype(jnp.bfloat16)
            for t in range(2):
                dst[s, t, c * BLK : (c + 1) * BLK, :] = jnp.dot(
                    hot, kv[t], preferred_element_type=jnp.float32
                ).astype(jnp.bfloat16)

    copies = [None]
    for s in range(1, row_devs):
        asks[s].wait_recv()
        pick(reqs, s, sends)
        copies.append(
            pltpu.make_async_remote_copy(
                sends.at[s], got_ref.at[s], kv_send.at[s], kv_recv.at[s], device_id=row_peer(-s), device_id_type=MESH
            )
        )
        copies[s].start()
    pick(want_ref, 0, got_ref)

    q = jnp.dot(x, w_ref[0], preferred_element_type=jnp.float32).reshape(rows // BLK, 2, HALF, width)
    top = q[:, 0].reshape(rows // 2, width)
    bottom = q[:, 1].reshape(rows // 2, width)
    first = lax.broadcasted_iota(jnp.int32, (rows // 2, 2 * HD), 1) < HD
    for pair in range(width // (2 * HD)):
        a = top[:, pair * 2 * HD : (pair + 1) * 2 * HD]
        b = bottom[:, pair * 2 * HD : (pair + 1) * 2 * HD]
        q_ref[2 * pair] = jnp.where(first, a, swap_halves(b)).astype(jnp.bfloat16)
        q_ref[2 * pair + 1] = jnp.where(first, swap_halves(a), b).astype(jnp.bfloat16)

    for s in range(1, row_devs):
        asks[s].wait_send()
        copies[s].wait()
    for s in range(1, head_devs):
        moves[s].wait()


def exchange(want, features, w_qkv, w_out, row_devs, head_devs):
    rows, depth = features.shape
    width = w_qkv.shape[2]
    vmem = pl.BlockSpec(memory_space=pltpu.VMEM)
    anywhere = pl.BlockSpec(memory_space=pltpu.HBM)
    dma = pltpu.SemaphoreType.DMA
    return pl.pallas_call(
        functools.partial(exchange_kernel, row_devs, head_devs),
        out_shape=[
            jax.ShapeDtypeStruct((width // HD, rows // 2, 2 * HD), jnp.bfloat16),
            jax.ShapeDtypeStruct((row_devs, 2, CAP * BLK, width), jnp.bfloat16),
            jax.ShapeDtypeStruct((head_devs, w_out.shape[0], w_out.shape[1] // head_devs), jnp.bfloat16),
        ],
        in_specs=[vmem, anywhere, anywhere, vmem],
        out_specs=[vmem] * 3,
        scratch_shapes=[
            pltpu.VMEM((rows, depth), jnp.bfloat16),
            pltpu.VMEM(w_qkv.shape, jnp.bfloat16),
            pltpu.VMEM((2, rows, width), jnp.bfloat16),
            pltpu.VMEM((row_devs, 8, 128), jnp.int32),
            pltpu.VMEM((row_devs, 2, CAP * BLK, width), jnp.bfloat16),
            dma((2,)),
            dma((row_devs,)),
            dma((row_devs,)),
            dma((row_devs,)),
            dma((row_devs,)),
            dma((head_devs,)),
            dma((head_devs,)),
        ],
        compiler_params=pltpu.CompilerParams(
            vmem_limit_bytes=60 * 2**20, collective_id=0, has_side_effects=True
        ),
        name="exchange",
    )(want, features, w_qkv, w_out)


def sums_kernel(heads, units, umap_ref, count_ref, gain_ref, bias_ref, t_ref, m_ref, tiles, best, acc):
    g = pl.program_id(0)
    count = count_ref[g]
    best[...] = jnp.full(best.shape, NEG, jnp.float32)
    acc[...] = jnp.zeros(acc.shape, jnp.float32)
    first = lax.broadcasted_iota(jnp.int32, (HALF, 2 * BLK), 1) < BLK

    def arrange(i, carry):
        for step in range(4):
            pair = i * 4 + step
            at = pl.multiple_of(pair * 2 * BLK, 2 * BLK)
            a = bias_ref[0, 0:HALF, pl.ds(at, 2 * BLK)].astype(jnp.float32)
            b = bias_ref[0, HALF:BLK, pl.ds(at, 2 * BLK)].astype(jnp.float32)
            for odd in range(2):
                j = 2 * pair + odd
                tile = jnp.where(first, swap_halves(a), b) if odd else jnp.where(first, a, swap_halves(b))
                tile = jnp.where(j < count, tile, NEG)
                tiles[j] = tile
                u = umap_ref[g, j]
                best[u] = jnp.maximum(best[u], tile)
        return carry

    lax.fori_loop(0, NB // 8, arrange, 0)
    gains = [gain_ref[h] * LOG2E for h in range(heads)]

    def add(i, carry):
        for step in range(8):
            j = i * 8 + step
            u = umap_ref[g, j]
            d = tiles[j] - best[u]
            e = [jnp.exp2(d * gains[h]) for h in range(heads)]
            for h in range(heads):
                acc[u, h] += e[h]
        return carry

    lax.fori_loop(0, (count + 7) // 8, add, 0)
    for u in range(units):
        m_ref[:, u * 2 * BLK : (u + 1) * 2 * BLK] = best[u].astype(jnp.bfloat16)
        for h in range(heads):
            t_ref[h, :, u * 2 * BLK : (u + 1) * 2 * BLK] = acc[u, h].astype(jnp.bfloat16)


def sums(umap, counts, bias_gain, edge_bias, units):
    blocks = umap.shape[0]
    heads = bias_gain.shape[0]
    wide = units * 2 * BLK
    rows2 = blocks * HALF
    grid_spec = pltpu.PrefetchScalarGridSpec(
        num_scalar_prefetch=3,
        grid=(blocks,),
        in_specs=[pl.BlockSpec((1, BLK, NB * BLK), lambda g, *_: (g, 0, 0))],
        out_specs=[
            pl.BlockSpec((heads, HALF, wide), lambda g, *_: (0, g, 0)),
            pl.BlockSpec((HALF, wide), lambda g, *_: (g, 0)),
        ],
        scratch_shapes=[
            pltpu.VMEM((NB, HALF, 2 * BLK), jnp.float32),
            pltpu.VMEM((units, HALF, 2 * BLK), jnp.float32),
            pltpu.VMEM((units, heads, HALF, 2 * BLK), jnp.float32),
        ],
    )
    return pl.pallas_call(
        functools.partial(sums_kernel, heads, units),
        out_shape=[
            jax.ShapeDtypeStruct((heads, rows2, wide), jnp.bfloat16),
            jax.ShapeDtypeStruct((rows2, wide), jnp.bfloat16),
        ],
        grid_spec=grid_spec,
        compiler_params=pltpu.CompilerParams(vmem_limit_bytes=60 * 2**20),
        cost_estimate=pl.CostEstimate(
            flops=10 * blocks * heads * BLK * NB * BLK * 100,
            bytes_accessed=12 * 2**20,
            transcendentals=blocks * heads * BLK * NB * BLK,
        ),
        name="sums",
    )(umap, counts, bias_gain, edge_bias)


def attend_kernel(
    row_devs, head_devs, gain_ref, q_ref, t_ref, m_ref, got_ref, wcol_ref, out_ref, att, send_sem, recv_sem
):
    z = lax.axis_index("head")
    peers = [{"head": lax.rem(z + s, head_devs)} for s in range(head_devs)]
    greet(peers[1:])
    units = CAP * row_devs
    rows2 = q_ref.shape[1]
    first_k = lax.broadcasted_iota(jnp.int32, (CAP * BLK, 2 * HD), 1) < HD
    first = lax.broadcasted_iota(jnp.int32, (rows2, 2 * HD), 1) < HD

    def doubled(part, pair, odd):
        rows = []
        for s in range(row_devs):
            x = got_ref[s, part, :, pair * 2 * HD : (pair + 1) * 2 * HD].astype(jnp.float32)
            y = swap_halves(x)
            low = jnp.where(first_k, y if odd else x, 0.0).astype(jnp.bfloat16)
            high = jnp.where(first_k, 0.0, x if odd else y).astype(jnp.bfloat16)
            for c in range(CAP):
                rows += [low[c * BLK : (c + 1) * BLK], high[c * BLK : (c + 1) * BLK]]
        return jnp.concatenate(rows, axis=0)

    def halves(x, op, fill):
        parts = [x[:, u * 2 * BLK : (u + 1) * 2 * BLK] for u in range(units)]
        while len(parts) > 1:
            parts = [op(parts[i], parts[i + 1]) for i in range(0, len(parts) - 1, 2)] + parts[len(parts) // 2 * 2 :]
        y = parts[0]
        reduce = jnp.max if op is jnp.maximum else jnp.sum
        low = reduce(jnp.where(first, y, fill), axis=1, keepdims=True)
        high = reduce(jnp.where(first, fill, y), axis=1, keepdims=True)
        return jnp.where(first, low, high)

    copies = []
    for pair in range(q_ref.shape[0] // 2):
        outs = []
        for odd in range(2):
            h = 2 * pair + odd
            gain = gain_ref[h] * LOG2E
            score = lax.dot_general(
                q_ref[h], doubled(0, pair, odd), (((1,), (1,)), ((), ())), preferred_element_type=jnp.float32
            )
            score = score * (HD**-0.5 * LOG2E) + m_ref[...].astype(jnp.float32) * gain
            top = halves(score, jnp.maximum, -jnp.inf)
            expo = jnp.exp2(score - jnp.concatenate([top] * units, axis=1)) * t_ref[h].astype(jnp.float32)
            total = halves(expo, jnp.add, 0.0)
            mixed = jnp.dot(expo.astype(jnp.bfloat16), doubled(1, pair, odd), preferred_element_type=jnp.float32)
            outs.append(mixed / total)
        a, b = outs
        lanes = slice(pair * 2 * HD, (pair + 1) * 2 * HD)
        att[0, 0, :, lanes] = jnp.where(first, a, swap_halves(b)).astype(jnp.bfloat16)
        att[0, 1, :, lanes] = jnp.where(first, swap_halves(a), b).astype(jnp.bfloat16)
        for s in range(1, head_devs):
            here = pl.ds(pair * 2 * HD, 2 * HD)
            copy = pltpu.make_async_remote_copy(
                att.at[0, :, :, here],
                att.at[s, :, :, here],
                send_sem.at[pair, s],
                recv_sem.at[pair, s],
                device_id=peers[head_devs - s],
                device_id_type=MESH,
            )
            copy.start()
            copies.append((s, copy))
    blocks, columns = out_ref.shape[0], out_ref.shape[3]
    total = [None, None]
    for s in range(head_devs):
        for shift, copy in copies:
            if shift == s:
                copy.wait_recv()
        for side in range(2):
            part = jnp.dot(att[s, side], wcol_ref[s], preferred_element_type=jnp.float32)
            total[side] = part if s == 0 else total[side] + part
    for side in range(2):
        out_ref[:, side] = total[side].reshape(blocks, HALF, columns).astype(jnp.bfloat16)
    for _, copy in copies:
        copy.wait_send()


def attend(bias_gain, q, t, m, got, wcol):
    heads, rows2, _ = q.shape
    head_devs, _, columns = wcol.shape
    vmem = pl.BlockSpec(memory_space=pltpu.VMEM)
    return pl.pallas_call(
        functools.partial(attend_kernel, got.shape[0], head_devs),
        out_shape=jax.ShapeDtypeStruct((rows2 // HALF, 2, HALF, columns), jnp.bfloat16),
        in_specs=[pl.BlockSpec(memory_space=pltpu.SMEM)] + [vmem] * 5,
        out_specs=vmem,
        scratch_shapes=[
            pltpu.VMEM((head_devs, 2, rows2, heads * HD), jnp.bfloat16),
            pltpu.SemaphoreType.DMA((heads // 2, head_devs)),
            pltpu.SemaphoreType.DMA((heads // 2, head_devs)),
        ],
        compiler_params=pltpu.CompilerParams(
            vmem_limit_bytes=60 * 2**20, collective_id=1, has_side_effects=True
        ),
        name="attend",
    )(bias_gain, q, t, m, got, wcol)


def body(features, w_qkv, w_out, bias_gain, edge_bias, neighbours, counts):
    rows = features.shape[0]
    blocks = rows // BLK
    row_devs = lax.axis_size("row")
    head_devs = lax.axis_size("head")
    me = lax.axis_index("row")
    units = CAP * row_devs

    owner, local = neighbours // blocks, neighbours % blocks
    hop = lax.rem(owner - me + row_devs, row_devs)
    hit = hop[None] == jnp.arange(row_devs, dtype=jnp.int32)[:, None, None]
    low = jnp.min(jnp.where(hit, local[None], blocks - 1), axis=(1, 2))
    high = jnp.max(jnp.where(hit, local[None], 0), axis=(1, 2))
    low_here = jnp.sum(jnp.where(hit, low[:, None, None], 0), axis=0)
    umap = CAP * hop + (local != low_here).astype(jnp.int32)
    wanted = jnp.stack([low, high], axis=1)
    want = jnp.broadcast_to(jnp.pad(wanted, ((0, 0), (0, 6)))[:, :, None], (row_devs, 8, 128))
    q, got, wcol = exchange(want, features, w_qkv, w_out, row_devs, head_devs)
    t, m = sums(umap, counts, bias_gain, edge_bias, units)
    out = attend(bias_gain, q, t, m, got, wcol)
    return out.reshape(rows, out.shape[3])


def solution(mesh):
    in_specs = (
        P("row", None),
        P(None, None, "head"),
        P("head", None),
        P("head"),
        P("row", None, None),
        P("row", None),
        P("row"),
    )
    return jax.shard_map(body, mesh=mesh, in_specs=in_specs, out_specs=P("row", "head"), check_vma=False)
```
